32 devices in a mesh: groups: 2 (over y), freq: 4 (over z), rows: 4 (over x, core).
Axes of the slice: x: 2, y: 2, z: 4, core: 2. Of those that a mesh axis runs over, the one named last changes fastest.
Arguments:
- traces: bfloat16 [8192, 32, 1024], P(('groups', 'freq'), 'rows'), parts along dimension 0, may hold values from -6 to 6
- tile_ranks: int32 [8, 16, 16], P(('groups', 'freq'), 'rows'), parts along dimension 0, may hold values from 8 to 32, as said below
- source_map: int32 [8192], P('groups'), parts along dimension 0, may hold values from 0 to 4095, as said below
- receiver_map: int32 [8192], P(('groups', 'rows')), parts along dimension 0, may hold values from 0 to 4095, as said below
- left_factors: float32 [2, 8, 16, 256, 512], P(None, ('groups', 'freq'), 'rows'), parts along dimension 1, may hold values from -0.3125 to 0.3125
- right_factors: float32 [2, 8, 16, 512, 256], P(None, ('groups', 'freq'), 'rows'), parts along dimension 1, may hold values from -0.375 to 0.375
Outputs:
- convolved: bfloat16 [8, 1024, 32, 1024], P(('groups', 'rows'), 'freq'), parts along dimension 0
The draws below stay inside these ranges and needn't reach their ends.
There are 2 independent parts, one for each index of `groups`. The reference program is written for one: setup_inputs(seed, part) draws one part's arguments, and reference() takes and returns one part's arrays. A program takes and returns all parts, laid end to end along the dimension named above; each array names one. Nothing has to cross between parts.
Inputs may be any that keep to these rules, and one draw needn't show every extreme that they name: `tile_ranks`: multiples of 8. For every frequency, the ranks of each tile row sum to at most 512, and some tile row has all its ranks equal to 32. `source_map`: A permutation of the slab's sources. `receiver_map`: each aligned block of 1024 entries is a permutation of that block's own indices.
All inputs are finite; a program needn't handle non-finite values.
Results may differ from the reference program's by a relative error of at most 0.0043.
Values sent between devices are 32-bit elements; how exact they have to be, the bound alone decides.
A program may use at most 192 MiB of HBM per device.

```python
import math
import jax
import jax.numpy as jnp
from jax import lax

TILE = 256
NTB = 16
NT = 1024
NV = 32
RMAX = 32
SLAB = 4096
NF = 4
RCAP = 512
RSH = 1024
N_ROWS = 4


def draw_tile_ranks(key, part):
    top_units = RMAX // 8
    key_high, key_bits, key_row = jax.random.split(key, 3)
    row_ceiling = jax.random.randint(key_high, (NF, NTB, 1), 2, top_units + 2)
    raw_bits = jax.random.randint(key_bits, (NF, NTB, NTB), 0, 1 << 20)
    rank_units = jnp.minimum(1 + raw_bits % row_ceiling, top_units)
    full_row = jax.random.randint(key_row, (NF, 1, 1), 0, NTB)
    row_index = jnp.arange(NTB).reshape(1, NTB, 1)
    rank_units = jnp.where(row_index == full_row, top_units, rank_units)
    return (8 * rank_units).astype(jnp.int32)


def draw_source_map(key, part):
    return jax.random.permutation(key, SLAB).astype(jnp.int32)


def draw_receiver_map(key, part):
    block_keys = jax.random.split(key, SLAB // RSH)
    block_perms = jax.vmap(lambda one_key: jax.random.permutation(one_key, RSH))(block_keys)
    offsets = (jnp.arange(SLAB // RSH) * RSH)[:, None]
    return (block_perms + offsets).reshape(SLAB).astype(jnp.int32)


def level_of(rng, dims, cuts, low, top_value):
    gain, own = 1.0, jax.random.fold_in(rng, 6)
    for position, blocks in cuts:
        heights = jnp.exp(jax.random.uniform(jax.random.fold_in(own, position), (blocks,), jnp.float32, low / len(cuts), top_value / len(cuts)))
        gain = gain * jnp.repeat(heights, dims[position] // blocks).reshape([-1 if axis == position else 1 for axis in range(len(dims))])
    return gain


def normal_values(rng, shape, spread, most, pieces=(), held_as=jnp.bfloat16):
    values = spread * jax.random.normal(rng, shape, jnp.float32)
    if pieces:
        values = values * level_of(rng, shape, pieces, -0.22, 0.18)
    return jnp.clip(values, -most, most).astype(held_as)


def setup_inputs(seed: int = 0, part: int = 0) -> dict:
    key_list = jax.random.split(jax.random.key(seed), 7)
    part_splits = jax.random.split(jax.random.fold_in(key_list[6], part), 7)
    traces = normal_values(part_splits[0], (SLAB, NV, NT), 1.0, 6.0, ((0, 4), (1, 4)))
    tile_ranks = draw_tile_ranks(jax.random.fold_in(jax.random.fold_in(key_list[6], part), 71), part)
    source_map = draw_source_map(jax.random.fold_in(jax.random.fold_in(key_list[6], part), 71), part)
    receiver_map = draw_receiver_map(jax.random.fold_in(jax.random.fold_in(key_list[6], part), 71), part)
    left_factors = normal_values(part_splits[4], (2, NF, NTB, TILE, RCAP), (24 * NTB) ** -0.5, 0.3125, ((1, 4), (2, 4)), jnp.float32)
    right_factors = normal_values(part_splits[5], (2, NF, NTB, RCAP, TILE), TILE ** -0.5, 0.375, ((1, 4), (2, 4)), jnp.float32)
    return {"traces": traces, "tile_ranks": tile_ranks, "source_map": source_map, "receiver_map": receiver_map, "left_factors": left_factors, "right_factors": right_factors}


def tables(samples, bins):
    sample_idx = jnp.arange(samples, dtype=jnp.int32)
    bin_idx = jnp.arange(bins, dtype=jnp.int32) + 1
    phase_turns = bin_idx[:, None] * sample_idx[None, :] % samples
    angles = phase_turns.astype(jnp.float32) * (2.0 * math.pi / samples)
    return jnp.stack([jnp.cos(angles), -jnp.sin(angles)], axis=1)

def slot_owner(row_ranks, slots):
    slot_ends = jnp.cumsum(row_ranks, axis=-1).astype(jnp.int32)
    starts = slot_ends - row_ranks
    slot_idx = jnp.arange(slots, dtype=jnp.int32)
    inside = (slot_idx[:, None] >= starts[..., None, :]) & (slot_idx[:, None] < slot_ends[..., None, :])
    return inside.astype(jnp.float32)

def reference(traces, tile_ranks, source_map, receiver_map, left_factors, right_factors):
    highest = lax.Precision.HIGHEST
    basis = tables(NT, NF)
    forward = (basis / math.sqrt(NT)).astype(jnp.bfloat16)
    spectra = jnp.einsum('fct,svt->fcvs', forward.astype(jnp.float32), traces.astype(jnp.float32), precision=highest)
    columns = jnp.take(spectra, source_map, axis=3)
    tile_size = SLAB // NTB

    def one_freq(packed_args):
        spectrum, rank_rows, left_one, right_one = packed_args
        source_matrix = spectrum.reshape(2, NV, NTB, tile_size).transpose(0, 3, 2, 1).reshape(2, tile_size, NTB * NV)
        owner = slot_owner(rank_rows, RCAP)
        proj_real = jnp.einsum('iks,sm->ikm', right_one[0], source_matrix[0], precision=highest) + jnp.einsum('iks,sm->ikm', right_one[1], source_matrix[1], precision=highest)
        proj_imag = jnp.einsum('iks,sm->ikm', right_one[0], source_matrix[1], precision=highest) - jnp.einsum('iks,sm->ikm', right_one[1], source_matrix[0], precision=highest)
        sel_real = jnp.einsum('ikjv,ikj->ikv', proj_real.reshape(NTB, RCAP, NTB, NV), owner, precision=highest)
        sel_imag = jnp.einsum('ikjv,ikj->ikv', proj_imag.reshape(NTB, RCAP, NTB, NV), owner, precision=highest)
        out_real = jnp.einsum('irk,ikv->irv', left_one[0], sel_real, precision=highest) - jnp.einsum('irk,ikv->irv', left_one[1], sel_imag, precision=highest)
        out_imag = jnp.einsum('irk,ikv->irv', left_one[0], sel_imag, precision=highest) + jnp.einsum('irk,ikv->irv', left_one[1], sel_real, precision=highest)
        return jnp.stack([out_real, out_imag]).reshape(2, SLAB, NV)
    image = lax.map(one_freq, (columns, tile_ranks, jnp.moveaxis(left_factors, 1, 0), jnp.moveaxis(right_factors, 1, 0)))
    image = jnp.take(image, receiver_map, axis=2)
    inverse = basis / math.sqrt(NF)
    waves = jnp.einsum('fcrv,fct->rvt', image, inverse, precision=highest)
    return waves.astype(jnp.bfloat16).reshape(N_ROWS, RSH, NV, NT)
```

```python
import functools
import math

import jax
import jax.numpy as jnp
import numpy as np
from jax import lax
from jax.experimental import pallas as pl
from jax.experimental.pallas import tpu as pltpu
from jax.sharding import PartitionSpec as P

RMAX = 32
MESH = pl.DeviceIdType.MESH
VMEM_LIMIT = 52 * 1024 * 1024


def tables(samples, bins):
    turns = (np.arange(bins)[:, None] + 1) * np.arange(samples)[None, :] % samples
    angles = turns.astype(np.float32) * np.float32(2.0 * math.pi / samples)
    return np.stack([np.cos(angles), -np.sin(angles)], axis=1).astype(np.float32)


def round_up(value, unit):
    return -(-value // unit) * unit


def row_messages(n_rows):
    known, messages = [0], []
    for bit in reversed(range(n_rows.bit_length() - 1)):
        messages += [(1 << bit, off) for off in known]
        known += [off ^ (1 << bit) for off in known]
    return messages


def spectra_kernel(nf, n_rows, chunks, x_ref, w_ref, t_ref, xbuf, sv, spec, land,
                   in_sem, s1_send, s1_recv, h_send, h_recv):
    z, r = lax.axis_index("freq"), lax.axis_index("rows")
    width, members = xbuf.shape[1], xbuf.shape[2]
    samples = xbuf.shape[3]
    lanes = w_ref.shape[1]
    sources = width * chunks
    messages = row_messages(n_rows)
    pair = 2 * members

    loads = []
    for c in range(chunks):
        load = pltpu.make_async_copy(x_ref.at[pl.ds(c * width, width)], xbuf.at[c], in_sem.at[c])
        load.start()
        loads.append(load)

    barrier = pltpu.get_barrier_semaphore()
    bits = [1 << b for b in range(n_rows.bit_length() - 1)]
    for d in range(1, nf):
        pl.semaphore_signal(barrier, inc=1, device_id={"freq": lax.rem(z + d, nf)}, device_id_type=MESH)
    for bit in bits:
        flip = r + bit - 2 * bit * lax.rem(r // bit, 2)
        pl.semaphore_signal(barrier, inc=1, device_id={"rows": flip}, device_id_type=MESH)
    pl.semaphore_wait(barrier, nf - 1 + len(bits))

    def flipped(index, mask):
        for bit in bits:
            if mask & bit:
                index = index + bit - 2 * bit * lax.rem(index // bit, 2)
        return index

    def band_copy(c, d):
        to = lax.rem(z + d, nf)
        return pltpu.make_async_remote_copy(
            src_ref=spec.at[c, to], dst_ref=land.at[c, r, z],
            send_sem=s1_send.at[c, d], recv_sem=s1_recv.at[c, d],
            device_id={"freq": to}, device_id_type=MESH)

    def row_copy(c, m):
        bit, off = messages[m]
        block = land.at[c, flipped(r, off)]
        return pltpu.make_async_remote_copy(
            src_ref=block, dst_ref=block,
            send_sem=h_send.at[c, m], recv_sem=h_recv.at[c, m],
            device_id={"rows": flipped(r, bit)}, device_id_type=MESH)

    def compute(c):
        piece = 128
        lane_v = lax.rem(lax.broadcasted_iota(jnp.int32, (piece, 128), 1), members)
        for s0 in range(0, width, piece):
            block = xbuf[c, s0:s0 + piece].reshape(piece * members, samples)
            found = jnp.dot(block, w_ref[...], preferred_element_type=jnp.float32)
            for tile in range(lanes // 128):
                sv[tile] = found[:, tile * 128:(tile + 1) * 128]
                picked = sv[tile, pl.ds(0, piece, stride=members), :]
                for v in range(1, members):
                    picked = jnp.where(lane_v == v, sv[tile, pl.ds(v, piece, stride=members), :], picked)
                turned = picked.T
                per_tile = 128 // pair
                for f in range(tile * per_tile, min(nf, (tile + 1) * per_tile)):
                    here = (f - tile * per_tile) * pair
                    spec[c, f, :, s0:s0 + piece] = turned[here:here + pair]
        land[c, r, z] = spec[c, z]
        for d in range(1, nf):
            band_copy(c, d).start()

    def turn(c):
        for zz in range(nf):
            parts = [land[c, rr, zz] for rr in range(n_rows)]
            again = []
            for part in parts:
                again += [-part[members:], part[:members]]
            full = jnp.concatenate(parts + again, axis=0)
            t_ref[zz * sources + c * width:zz * sources + (c + 1) * width, :] = full.T

    stages = []
    for m, (bit, off) in enumerate(messages):
        stage = 0 if off == 0 else bits.__len__() - (off & -off).bit_length() + 1
        stages.append(stage)
    depth = len(bits)
    for step in range(chunks + depth + 1):
        if step < chunks:
            loads[step].wait()
            compute(step)
        for stage in range(depth + 1):
            c = step - 1 - stage
            if not 0 <= c < chunks:
                continue
            if stage == 0:
                for d in range(1, nf):
                    band_copy(c, d).wait_recv()
            else:
                done_bit = bits[depth - stage]
                for m, (bit, off) in enumerate(messages):
                    if bit == done_bit:
                        row_copy(c, m).wait_recv()
            for m in range(len(messages)):
                if stages[m] == stage:
                    row_copy(c, m).start()
            if stage == depth:
                turn(c)
    for c in range(chunks):
        for d in range(1, nf):
            band_copy(c, d).wait_send()
        for m in range(len(messages)):
            row_copy(c, m).wait_send()


def image_kernel(t_ref, smap, rmap, ranks, left, right, o_ref, cols, lbuf, rbuf, proj, img, even, odd, l_sem, r_sem):
    slab = cols.shape[0]
    tile_rows, blocks = ranks.shape[1], ranks.shape[2]
    capacity, tile = right.shape[3], right.shape[4]
    receivers = img.shape[0]
    loads_r = [[pltpu.make_async_copy(right.at[c, 0, i], rbuf.at[c, i, pl.ds(0, capacity)], r_sem.at[c, i])
                for i in range(tile_rows)] for c in range(2)]
    loads_l = [[pltpu.make_async_copy(left.at[c, 0, i], lbuf.at[c, i], l_sem.at[c, i])
                for i in range(tile_rows)] for c in range(2)]
    for loads in (loads_r, loads_l):
        for i in range(tile_rows):
            for c in range(2):
                loads[c][i].start()
    proj[...] = jnp.zeros_like(proj)

    @pl.loop(0, slab // 16)
    def _(g):
        for u in range(16):
            q = g * 16 + u
            cols[pl.ds(q, 1), :] = t_ref[pl.ds(smap[q], 1), :]

    for i in range(tile_rows):
        for c in range(2):
            loads_r[c][i].wait()
    lane = lax.broadcasted_iota(jnp.int32, (tile_rows * RMAX, 128), 1)
    sign = jnp.where(lane < 64, -1.0, 1.0)
    starts = [jnp.int32(0)] * tile_rows
    for j in range(blocks):
        col = cols[j * tile:(j + 1) * tile, :].astype(jnp.bfloat16)
        at = [pl.multiple_of(s, 8) for s in starts]
        both = [jnp.concatenate([rbuf[c, i, pl.ds(at[i], RMAX), :] for i in range(tile_rows)], axis=0)
                .astype(jnp.bfloat16) for c in range(2)]
        first = jnp.dot(both[0], col, preferred_element_type=jnp.float32)
        second = jnp.dot(both[1], col, preferred_element_type=jnp.float32)
        total = first + sign * pltpu.roll(second, 64, 1)
        for i in range(tile_rows):
            proj[i, pl.ds(at[i], RMAX), :] = total[i * RMAX:(i + 1) * RMAX]
            starts[i] = starts[i] + ranks[0, i, j]
    for i in range(tile_rows):
        proj[i, pl.ds(pl.multiple_of(starts[i], 8), RMAX), :] = jnp.zeros((RMAX, 128), jnp.float32)
    for i in range(tile_rows):
        p = proj[i, :capacity, :]
        high = p.astype(jnp.bfloat16)
        low = (p - high.astype(jnp.float32)).astype(jnp.bfloat16)
        wide = jnp.concatenate([high, low], axis=1)
        sums = []
        for c in range(2):
            loads_l[c][i].wait()
            prod = jnp.dot(lbuf[c, i].astype(jnp.bfloat16), wide, preferred_element_type=jnp.float32)
            sums.append(prod[:, :128] + prod[:, 128:])
        img[i * tile:(i + 1) * tile, :] = sums[0] + pltpu.roll(sums[1], 64, 1)

    @pl.loop(0, receivers // 16)
    def _(g):
        for u in range(8):
            n = g * 16 + 2 * u
            even[pl.ds(g * 8 + u, 1), :] = img[pl.ds(lax.rem(rmap[n], receivers), 1), :]
            odd[pl.ds(g * 8 + u, 1), :] = img[pl.ds(lax.rem(rmap[n + 1], receivers), 1), :]

    lane2 = lax.broadcasted_iota(jnp.int32, even.shape, 1)
    o_ref[...] = jnp.where(lane2 < 64, even[...], pltpu.roll(odd[...], 64, 1)).reshape(o_ref.shape)


def return_kernel(nf, i_ref, o_ref, own_sem, send_sem, recv_sem):
    z = lax.axis_index("freq")
    own = pltpu.make_async_copy(i_ref.at[z], o_ref.at[z], own_sem)
    own.start()
    barrier = pltpu.get_barrier_semaphore()
    for d in range(1, nf):
        pl.semaphore_signal(barrier, inc=1, device_id={"freq": lax.rem(z + d, nf)}, device_id_type=MESH)
    pl.semaphore_wait(barrier, nf - 1)
    copies = []
    for d in range(1, nf):
        to = lax.rem(z + d, nf)
        copy = pltpu.make_async_remote_copy(
            src_ref=i_ref.at[to], dst_ref=o_ref.at[z],
            send_sem=send_sem.at[d], recv_sem=recv_sem.at[d],
            device_id={"freq": to}, device_id_type=MESH)
        copy.start()
        copies.append(copy)
    own.wait()
    for copy in copies:
        copy.wait()


def waves_kernel(nf, members, x_ref, w_ref, o_ref, rows, lhs):
    pairs = x_ref.shape[1]
    wide = w_ref.shape[0]
    groups = members // 8
    lane = lax.broadcasted_iota(jnp.int32, (pairs, 128), 1)
    units = [(part, f) for part in (0, 0, 1) for f in range(nf)]
    pieces = []
    for f in range(nf):
        x = x_ref[f]
        high = x.astype(jnp.bfloat16).astype(jnp.float32)
        pieces.append((high, x - high))
    for parity in range(2):
        for g in range(groups):
            base = 64 * parity + 16 * g
            for tile in range(wide // 128):
                acc = jnp.zeros((pairs, 128), jnp.float32)
                for slot, (part, f) in enumerate(units[tile * 8:tile * 8 + 8]):
                    shift = (16 * slot - base) % 128
                    value = pieces[f][part]
                    if shift:
                        value = pltpu.roll(value, shift, 1)
                    acc = jnp.where(lane // 16 == slot, value, acc)
                rows[parity, g, :, tile * 128:tile * 128 + 128] = acc
    sub = lax.broadcasted_iota(jnp.int32, (8, wide), 0)
    keep = lax.rem(lax.broadcasted_iota(jnp.int32, (8, wide), 1), 8) == sub
    for n in range(2 * pairs):
        parts = []
        for g in range(groups):
            row = rows[n % 2, g, pl.ds(n // 2, 1), :]
            parts.append(jnp.where(keep, jnp.broadcast_to(row, (8, wide)), 0.0))
        lhs[n * members:(n + 1) * members, :] = jnp.concatenate(parts, axis=0).astype(jnp.bfloat16)
    step = 4
    for n in range(0, 2 * pairs, step):
        out = jnp.dot(lhs[n * members:(n + step) * members, :], w_ref[...], preferred_element_type=jnp.float32)
        o_ref[0, n:n + step] = out.astype(jnp.bfloat16).reshape(step, members, out.shape[1])


def per_device(traces, tile_ranks, source_map, receiver_map, left_factors, right_factors):
    sources, members, samples = traces.shape
    nf, n_rows = lax.axis_size("freq"), lax.axis_size("rows")
    slab = source_map.shape[0]
    receivers = receiver_map.shape[0]
    all_members = members * n_rows
    tile_rows, capacity, tile = right_factors.shape[2:]
    chunks = max(1, sources // 256)
    width = sources // chunks
    basis = tables(samples, nf)

    forward = (basis / np.float32(math.sqrt(samples))).astype(jnp.bfloat16)
    lanes = round_up(2 * nf * members, 128)
    w = np.zeros((samples, lanes), jnp.bfloat16)
    w[:, :2 * nf * members] = np.repeat(forward.reshape(2 * nf, samples), members, axis=0).T
    n_msg = n_rows - 1
    turned = pl.pallas_call(
        functools.partial(spectra_kernel, nf, n_rows, chunks),
        out_shape=jax.ShapeDtypeStruct((slab, 128), jnp.float32),
        in_specs=[pl.BlockSpec(memory_space=pl.ANY), pl.BlockSpec(memory_space=pltpu.VMEM)],
        out_specs=pl.BlockSpec(memory_space=pltpu.VMEM),
        scratch_shapes=[
            pltpu.VMEM((chunks, width, members, samples), jnp.bfloat16),
            pltpu.VMEM((lanes // 128, 128 * members, 128), jnp.float32),
            pltpu.VMEM((chunks, nf, 2 * members, width), jnp.float32),
            pltpu.VMEM((chunks, n_rows, nf, 2 * members, width), jnp.float32),
            pltpu.SemaphoreType.DMA((chunks,)),
            pltpu.SemaphoreType.DMA((chunks, nf)),
            pltpu.SemaphoreType.DMA((chunks, nf)),
            pltpu.SemaphoreType.DMA((chunks, n_msg)),
            pltpu.SemaphoreType.DMA((chunks, n_msg)),
        ],
        compiler_params=pltpu.CompilerParams(
            collective_id=0, has_side_effects=True, vmem_limit_bytes=VMEM_LIMIT),
        name="spectra",
    )(traces, jnp.asarray(w))

    per = receivers // nf
    image = pl.pallas_call(
        image_kernel,
        out_shape=jax.ShapeDtypeStruct((nf, per // 2, 128), jnp.float32),
        in_specs=[
            pl.BlockSpec(memory_space=pltpu.VMEM),
            pl.BlockSpec(memory_space=pltpu.SMEM),
            pl.BlockSpec(memory_space=pltpu.SMEM),
            pl.BlockSpec(memory_space=pltpu.SMEM),
            pl.BlockSpec(memory_space=pl.ANY),
            pl.BlockSpec(memory_space=pl.ANY),
        ],
        out_specs=pl.BlockSpec(memory_space=pltpu.VMEM),
        scratch_shapes=[
            pltpu.VMEM((slab, 128), jnp.float32),
            pltpu.VMEM((2, tile_rows, tile, capacity), jnp.float32),
            pltpu.VMEM((2, tile_rows, capacity + RMAX, tile), jnp.float32),
            pltpu.VMEM((tile_rows, capacity + RMAX, 128), jnp.float32),
            pltpu.VMEM((receivers, 128), jnp.float32),
            pltpu.VMEM((receivers // 2, 128), jnp.float32),
            pltpu.VMEM((receivers // 2, 128), jnp.float32),
            pltpu.SemaphoreType.DMA((2, tile_rows)),
            pltpu.SemaphoreType.DMA((2, tile_rows)),
        ],
        compiler_params=pltpu.CompilerParams(vmem_limit_bytes=VMEM_LIMIT),
        name="image",
    )(turned, source_map, receiver_map, tile_ranks, left_factors, right_factors)

    returned = pl.pallas_call(
        functools.partial(return_kernel, nf),
        out_shape=jax.ShapeDtypeStruct(image.shape, jnp.float32),
        in_specs=[pl.BlockSpec(memory_space=pltpu.VMEM)],
        out_specs=pl.BlockSpec(memory_space=pltpu.VMEM),
        scratch_shapes=[
            pltpu.SemaphoreType.DMA(()),
            pltpu.SemaphoreType.DMA((nf,)),
            pltpu.SemaphoreType.DMA((nf,)),
        ],
        compiler_params=pltpu.CompilerParams(collective_id=1, has_side_effects=True),
        name="giveback",
    )(image)

    inverse = (basis / np.float32(math.sqrt(nf))).astype(np.float32)
    high = inverse.astype(jnp.bfloat16)
    low = (inverse - high.astype(np.float32)).astype(jnp.bfloat16)
    wide = round_up(3 * nf * 16, 128)
    wb = np.zeros((wide, samples), jnp.bfloat16)
    for part, table in enumerate((high, low, high)):
        wb[part * nf * 16:(part + 1) * nf * 16] = np.repeat(table.reshape(2 * nf, samples), 8, axis=0)
    nb = 16
    return pl.pallas_call(
        functools.partial(waves_kernel, nf, all_members),
        grid=(per // nb,),
        out_shape=jax.ShapeDtypeStruct((1, per, all_members, samples), jnp.bfloat16),
        in_specs=[
            pl.BlockSpec((nf, nb // 2, 128), lambda i: (0, i, 0)),
            pl.BlockSpec((wide, samples), lambda i: (0, 0)),
        ],
        out_specs=pl.BlockSpec((1, nb, all_members, samples), lambda i: (0, i, 0, 0)),
        scratch_shapes=[
            pltpu.VMEM((2, all_members // 8, nb // 2, wide), jnp.float32),
            pltpu.VMEM((nb * all_members, wide), jnp.bfloat16),
        ],
        compiler_params=pltpu.CompilerParams(vmem_limit_bytes=VMEM_LIMIT),
        name="waves",
    )(returned, jnp.asarray(wb))


def solution(mesh):
    return jax.shard_map(
        per_device,
        mesh=mesh,
        in_specs=(
            P(("groups", "freq"), "rows", None),
            P(("groups", "freq"), "rows", None),
            P("groups"),
            P(("groups", "rows")),
            P(None, ("groups", "freq"), "rows", None, None),
            P(None, ("groups", "freq"), "rows", None, None),
        ),
        out_specs=P(("groups", "rows"), "freq", None, None),
        check_vma=False,
    )
```

```python
import functools
import math

import jax
import jax.numpy as jnp
import numpy as np
from jax import lax
from jax.experimental import pallas as pl
from jax.experimental.pallas import tpu as pltpu
from jax.sharding import PartitionSpec as P

RMAX = 32
MESH = pl.DeviceIdType.MESH
VMEM_LIMIT = 52 * 1024 * 1024


def tables(samples, bins):
    turns = (np.arange(bins)[:, None] + 1) * np.arange(samples)[None, :] % samples
    angles = turns.astype(np.float32) * np.float32(2.0 * math.pi / samples)
    return np.stack([np.cos(angles), -np.sin(angles)], axis=1).astype(np.float32)


def round_up(value, unit):
    return -(-value // unit) * unit


def row_messages(n_rows):
    known, messages = [0], []
    for bit in reversed(range(n_rows.bit_length() - 1)):
        messages += [(1 << bit, off) for off in known]
        known += [off ^ (1 << bit) for off in known]
    return messages


def spectra_kernel(nf, n_rows, chunks, x_ref, w_ref, t_ref, xbuf, sv, spec, land,
                   in_sem, s1_send, s1_recv, h_send, h_recv):
    z, r = lax.axis_index("freq"), lax.axis_index("rows")
    width, members = xbuf.shape[1], xbuf.shape[2]
    samples = xbuf.shape[3]
    lanes = w_ref.shape[1]
    sources = width * chunks
    messages = row_messages(n_rows)
    pair = 2 * members

    loads = []
    for c in range(chunks):
        load = pltpu.make_async_copy(x_ref.at[pl.ds(c * width, width)], xbuf.at[c], in_sem.at[c])
        loads.append(load)

    barrier = pltpu.get_barrier_semaphore()
    bits = [1 << b for b in range(n_rows.bit_length() - 1)]
    for d in range(1, nf):
        pl.semaphore_signal(barrier, inc=1, device_id={"freq": lax.rem(z + d, nf)}, device_id_type=MESH)
    for bit in bits:
        flip = r + bit - 2 * bit * lax.rem(r // bit, 2)
        pl.semaphore_signal(barrier, inc=1, device_id={"rows": flip}, device_id_type=MESH)
    pl.semaphore_wait(barrier, nf - 1 + len(bits))

    def flipped(index, mask):
        for bit in bits:
            if mask & bit:
                index = index + bit - 2 * bit * lax.rem(index // bit, 2)
        return index

    def band_copy(c, d):
        to = lax.rem(z + d, nf)
        return pltpu.make_async_remote_copy(
            src_ref=spec.at[c, to], dst_ref=land.at[c, r, z],
            send_sem=s1_send.at[c, d], recv_sem=s1_recv.at[c, d],
            device_id={"freq": to}, device_id_type=MESH)

    def row_copy(c, m, d):
        bit, off = messages[m]
        block = land.at[c, flipped(r, off), lax.rem(z - d + nf, nf)]
        return pltpu.make_async_remote_copy(
            src_ref=block, dst_ref=block,
            send_sem=h_send.at[c, m, d], recv_sem=h_recv.at[c, m, d],
            device_id={"rows": flipped(r, bit)}, device_id_type=MESH)

    first_hop = [m for m, (bit, off) in enumerate(messages) if off == 0]

    def compute(c):
        piece = 128
        lane_v = lax.rem(lax.broadcasted_iota(jnp.int32, (piece, 128), 1), members)
        for s0 in range(0, width, piece):
            block = xbuf[c, s0:s0 + piece].reshape(piece * members, samples)
            found = jnp.dot(block, w_ref[...], preferred_element_type=jnp.float32)
            for tile in range(lanes // 128):
                sv[tile] = found[:, tile * 128:(tile + 1) * 128]
                picked = sv[tile, pl.ds(0, piece, stride=members), :]
                for v in range(1, members):
                    picked = jnp.where(lane_v == v, sv[tile, pl.ds(v, piece, stride=members), :], picked)
                turned = picked.T
                per_tile = 128 // pair
                for f in range(tile * per_tile, min(nf, (tile + 1) * per_tile)):
                    here = (f - tile * per_tile) * pair
                    spec[c, f, :, s0:s0 + piece] = turned[here:here + pair]
        land[c, r, z] = spec[c, z]
        for d in range(1, nf):
            band_copy(c, d).start()
        for m in first_hop:
            row_copy(c, m, 0).start()

    def turn(c):
        for zz in range(nf):
            parts = [land[c, rr, zz] for rr in range(n_rows)]
            again = []
            for part in parts:
                again += [-part[members:], part[:members]]
            full = jnp.concatenate(parts + again, axis=0)
            t_ref[zz * sources + c * width:zz * sources + (c + 1) * width, :] = full.T

    depth = len(bits)
    order = list(reversed(bits))
    forward = [[m for m, (bit, off) in enumerate(messages) if off and (off & -off) == order[k]] for k in range(depth)]

    def stage(k, c):
        if k == 0:
            for d in range(1, nf):
                band_copy(c, d).wait_recv()
                for m in first_hop:
                    row_copy(c, m, d).start()
            return
        for d in range(nf):
            for m, (bit, off) in enumerate(messages):
                if bit == order[k - 1]:
                    row_copy(c, m, d).wait_recv()
            for m in forward[k - 1]:
                row_copy(c, m, d).start()

    ahead = min(2, chunks)
    for c in range(ahead):
        loads[c].start()
    for step in range(chunks + depth + 3):
        if step < chunks:
            loads[step].wait()
            compute(step)
            if step + ahead < chunks:
                loads[step + ahead].start()
        for k in range(depth + 1):
            c = step - 2 - (k + 1 if k else 0)
            if 0 <= c < chunks:
                stage(k, c)
                if k == depth:
                    turn(c)
    for c in range(chunks):
        for d in range(nf):
            if d:
                band_copy(c, d).wait_send()
            for m in range(len(messages)):
                row_copy(c, m, d).wait_send()


def project_kernel(t_ref, smap, ranks, right, o_ref, cols, rbuf, proj, r_sem):
    slab = cols.shape[0]
    tile_rows, blocks = ranks.shape[1], ranks.shape[2]
    capacity, tile = right.shape[3], right.shape[4]
    loads_r = [[pltpu.make_async_copy(right.at[c, 0, i], rbuf.at[c, i, pl.ds(0, capacity)], r_sem.at[c, i])
                for i in range(tile_rows)] for c in range(2)]
    for i in range(tile_rows):
        for c in range(2):
            loads_r[c][i].start()
    proj[...] = jnp.zeros_like(proj)

    @pl.loop(0, slab // 32)
    def _(g):
        for u in range(32):
            q = g * 32 + u
            cols[pl.ds(q, 1), :] = t_ref[pl.ds(smap[q], 1), :]

    for i in range(tile_rows):
        for c in range(2):
            loads_r[c][i].wait()
    lane = lax.broadcasted_iota(jnp.int32, (tile_rows * RMAX, 128), 1)
    sign = jnp.where(lane < 64, -1.0, 1.0)
    starts = [jnp.int32(0)] * tile_rows
    for j in range(blocks):
        col = cols[j * tile:(j + 1) * tile, :].astype(jnp.bfloat16)
        at = [pl.multiple_of(s, 8) for s in starts]
        both = [jnp.concatenate([rbuf[c, i, pl.ds(at[i], RMAX), :] for i in range(tile_rows)], axis=0)
                .astype(jnp.bfloat16) for c in range(2)]
        first = jnp.dot(both[0], col, preferred_element_type=jnp.float32)
        second = jnp.dot(both[1], col, preferred_element_type=jnp.float32)
        total = first + sign * pltpu.roll(second, 64, 1)
        for i in range(tile_rows):
            proj[i, pl.ds(at[i], RMAX), :] = total[i * RMAX:(i + 1) * RMAX]
            starts[i] = starts[i] + ranks[0, i, j]
    for i in range(tile_rows):
        proj[i, pl.ds(pl.multiple_of(starts[i], 8), RMAX), :] = jnp.zeros((RMAX, 128), jnp.float32)
    for i in range(tile_rows):
        o_ref[i] = proj[i, :capacity, :]


def image_kernel(nf, p_ref, rmap, left, o_ref, lbuf, img, even, odd, out, l_sem, own_sem, send_sem, recv_sem):
    z = lax.axis_index("freq")
    tile_rows, tile = lbuf.shape[1], lbuf.shape[2]
    receivers = img.shape[0]
    pairs = out.shape[1]
    loads_l = [[pltpu.make_async_copy(left.at[c, 0, i], lbuf.at[c, i], l_sem.at[c, i])
                for i in range(tile_rows)] for c in range(2)]
    for i in range(tile_rows):
        for c in range(2):
            loads_l[c][i].start()
    barrier = pltpu.get_barrier_semaphore()
    for d in range(1, nf):
        pl.semaphore_signal(barrier, inc=1, device_id={"freq": lax.rem(z + d, nf)}, device_id_type=MESH)
    for i in range(tile_rows):
        p = p_ref[i]
        high = p.astype(jnp.bfloat16)
        low = (p - high.astype(jnp.float32)).astype(jnp.bfloat16)
        wide = jnp.concatenate([high, low], axis=1)
        sums = []
        for c in range(2):
            loads_l[c][i].wait()
            prod = jnp.dot(lbuf[c, i].astype(jnp.bfloat16), wide, preferred_element_type=jnp.float32)
            sums.append(prod[:, :128] + prod[:, 128:])
        img[i * tile:(i + 1) * tile, :] = sums[0] + pltpu.roll(sums[1], 64, 1)
    pl.semaphore_wait(barrier, nf - 1)

    copies = []
    lane2 = lax.broadcasted_iota(jnp.int32, (pairs, 128), 1)
    for d in list(range(1, nf)) + [0]:
        to = lax.rem(z + d, nf)
        first = to * 2 * pairs

        @pl.loop(0, pairs // 8)
        def _(g):
            for u in range(8):
                n = first + g * 16 + 2 * u
                even[d, pl.ds(g * 8 + u, 1), :] = img[pl.ds(lax.rem(rmap[n], receivers), 1), :]
                odd[d, pl.ds(g * 8 + u, 1), :] = img[pl.ds(lax.rem(rmap[n + 1], receivers), 1), :]

        out[d] = jnp.where(lane2 < 64, even[d], pltpu.roll(odd[d], 64, 1))
        if d:
            copy = pltpu.make_async_remote_copy(
                src_ref=out.at[d], dst_ref=o_ref.at[z],
                send_sem=send_sem.at[d], recv_sem=recv_sem.at[d],
                device_id={"freq": to}, device_id_type=MESH)
        else:
            copy = pltpu.make_async_copy(out.at[0], o_ref.at[z], own_sem)
        copy.start()
        copies.append(copy)
    for copy in copies:
        copy.wait()


def waves_kernel(nf, members, x_ref, w_ref, o_ref, rows, lhs):
    pairs = x_ref.shape[1]
    wide = w_ref.shape[0]
    groups = members // 8
    lane = lax.broadcasted_iota(jnp.int32, (pairs, 128), 1)
    units = [(part, f) for part in (0, 0, 1) for f in range(nf)]
    pieces = []
    for f in range(nf):
        x = x_ref[f]
        high = x.astype(jnp.bfloat16).astype(jnp.float32)
        pieces.append((high, x - high))
    for parity in range(2):
        for g in range(groups):
            base = 64 * parity + 16 * g
            for tile in range(wide // 128):
                acc = jnp.zeros((pairs, 128), jnp.float32)
                for slot, (part, f) in enumerate(units[tile * 8:tile * 8 + 8]):
                    shift = (16 * slot - base) % 128
                    value = pieces[f][part]
                    if shift:
                        value = pltpu.roll(value, shift, 1)
                    acc = jnp.where(lane // 16 == slot, value, acc)
                rows[parity, g, :, tile * 128:tile * 128 + 128] = acc
    sub = lax.broadcasted_iota(jnp.int32, (8, wide), 0)
    keep = lax.rem(lax.broadcasted_iota(jnp.int32, (8, wide), 1), 8) == sub
    half = pairs * members
    cut = min(256, w_ref.shape[1])
    for first in (0, pairs):
        for n in range(first, first + pairs):
            parts = []
            for g in range(groups):
                row = rows[n % 2, g, pl.ds(n // 2, 1), :]
                parts.append(jnp.where(keep, jnp.broadcast_to(row, (8, wide)), 0.0))
            lhs[n * members:(n + 1) * members, :] = jnp.concatenate(parts, axis=0).astype(jnp.bfloat16)
        block = lhs[first * members:first * members + half, :]
        for t in range(0, w_ref.shape[1], cut):
            out = jnp.dot(block, w_ref[:, t:t + cut], preferred_element_type=jnp.float32)
            o_ref[0, first:first + pairs, :, t:t + cut] = out.astype(jnp.bfloat16).reshape(pairs, members, cut)


def per_device(traces, tile_ranks, source_map, receiver_map, left_factors, right_factors):
    sources, members, samples = traces.shape
    nf, n_rows = lax.axis_size("freq"), lax.axis_size("rows")
    slab = source_map.shape[0]
    receivers = receiver_map.shape[0]
    all_members = members * n_rows
    tile_rows, capacity, tile = right_factors.shape[2:]
    chunks = max(1, sources // 256)
    width = sources // chunks
    basis = tables(samples, nf)

    forward = (basis / np.float32(math.sqrt(samples))).astype(jnp.bfloat16)
    lanes = round_up(2 * nf * members, 128)
    w = np.zeros((samples, lanes), jnp.bfloat16)
    w[:, :2 * nf * members] = np.repeat(forward.reshape(2 * nf, samples), members, axis=0).T
    n_msg = n_rows - 1
    turned = pl.pallas_call(
        functools.partial(spectra_kernel, nf, n_rows, chunks),
        out_shape=jax.ShapeDtypeStruct((slab, 128), jnp.float32),
        in_specs=[pl.BlockSpec(memory_space=pl.ANY), pl.BlockSpec(memory_space=pltpu.VMEM)],
        out_specs=pl.BlockSpec(memory_space=pltpu.VMEM),
        scratch_shapes=[
            pltpu.VMEM((chunks, width, members, samples), jnp.bfloat16),
            pltpu.VMEM((lanes // 128, 128 * members, 128), jnp.float32),
            pltpu.VMEM((chunks, nf, 2 * members, width), jnp.float32),
            pltpu.VMEM((chunks, n_rows, nf, 2 * members, width), jnp.float32),
            pltpu.SemaphoreType.DMA((chunks,)),
            pltpu.SemaphoreType.DMA((chunks, nf)),
            pltpu.SemaphoreType.DMA((chunks, nf)),
            pltpu.SemaphoreType.DMA((chunks, n_msg, nf)),
            pltpu.SemaphoreType.DMA((chunks, n_msg, nf)),
        ],
        compiler_params=pltpu.CompilerParams(
            collective_id=0, has_side_effects=True, vmem_limit_bytes=VMEM_LIMIT),
        name="spectra",
    )(traces, jnp.asarray(w))

    per = receivers // nf
    projected = pl.pallas_call(
        project_kernel,
        out_shape=jax.ShapeDtypeStruct((tile_rows, capacity, 128), jnp.float32),
        in_specs=[
            pl.BlockSpec(memory_space=pltpu.VMEM),
            pl.BlockSpec(memory_space=pltpu.SMEM),
            pl.BlockSpec(memory_space=pltpu.SMEM),
            pl.BlockSpec(memory_space=pl.ANY),
        ],
        out_specs=pl.BlockSpec(memory_space=pltpu.VMEM),
        scratch_shapes=[
            pltpu.VMEM((slab, 128), jnp.float32),
            pltpu.VMEM((2, tile_rows, capacity + RMAX, tile), jnp.float32),
            pltpu.VMEM((tile_rows, capacity + RMAX, 128), jnp.float32),
            pltpu.SemaphoreType.DMA((2, tile_rows)),
        ],
        compiler_params=pltpu.CompilerParams(vmem_limit_bytes=VMEM_LIMIT),
        name="project",
    )(turned, source_map, tile_ranks, right_factors)

    pairs = per // 2
    returned = pl.pallas_call(
        functools.partial(image_kernel, nf),
        out_shape=jax.ShapeDtypeStruct((nf, pairs, 128), jnp.float32),
        in_specs=[
            pl.BlockSpec(memory_space=pltpu.VMEM),
            pl.BlockSpec(memory_space=pltpu.SMEM),
            pl.BlockSpec(memory_space=pl.ANY),
        ],
        out_specs=pl.BlockSpec(memory_space=pl.ANY),
        scratch_shapes=[
            pltpu.VMEM((2, tile_rows, tile, capacity), jnp.float32),
            pltpu.VMEM((receivers, 128), jnp.float32),
            pltpu.VMEM((nf, pairs, 128), jnp.float32),
            pltpu.VMEM((nf, pairs, 128), jnp.float32),
            pltpu.VMEM((nf, pairs, 128), jnp.float32),
            pltpu.SemaphoreType.DMA((2, tile_rows)),
            pltpu.SemaphoreType.DMA(()),
            pltpu.SemaphoreType.DMA((nf,)),
            pltpu.SemaphoreType.DMA((nf,)),
        ],
        compiler_params=pltpu.CompilerParams(
            collective_id=1, has_side_effects=True, vmem_limit_bytes=VMEM_LIMIT),
        name="image",
    )(projected, receiver_map, left_factors)

    inverse = (basis / np.float32(math.sqrt(nf))).astype(np.float32)
    high = inverse.astype(jnp.bfloat16)
    low = (inverse - high.astype(np.float32)).astype(jnp.bfloat16)
    wide = round_up(3 * nf * 16, 128)
    wb = np.zeros((wide, samples), jnp.bfloat16)
    for part, table in enumerate((high, low, high)):
        wb[part * nf * 16:(part + 1) * nf * 16] = np.repeat(table.reshape(2 * nf, samples), 8, axis=0)
    nb = min(64, per)
    return pl.pallas_call(
        functools.partial(waves_kernel, nf, all_members),
        grid=(per // nb,),
        out_shape=jax.ShapeDtypeStruct((1, per, all_members, samples), jnp.bfloat16),
        in_specs=[
            pl.BlockSpec((nf, nb // 2, 128), lambda i: (0, i, 0)),
            pl.BlockSpec((wide, samples), lambda i: (0, 0)),
        ],
        out_specs=pl.BlockSpec((1, nb, all_members, samples), lambda i: (0, i, 0, 0)),
        scratch_shapes=[
            pltpu.VMEM((2, all_members // 8, nb // 2, wide), jnp.float32),
            pltpu.VMEM((nb * all_members, wide), jnp.bfloat16),
        ],
        compiler_params=pltpu.CompilerParams(vmem_limit_bytes=VMEM_LIMIT),
        name="waves",
    )(returned, jnp.asarray(wb))


def solution(mesh):
    return jax.shard_map(
        per_device,
        mesh=mesh,
        in_specs=(
            P(("groups", "freq"), "rows", None),
            P(("groups", "freq"), "rows", None),
            P("groups"),
            P(("groups", "rows")),
            P(None, ("groups", "freq"), "rows", None, None),
            P(None, ("groups", "freq"), "rows", None, None),
        ),
        out_specs=P(("groups", "rows"), "freq", None, None),
        check_vma=False,
    )
```

```python
import functools
import math

import jax
import jax.numpy as jnp
import numpy as np
from jax import lax
from jax.experimental import pallas as pl
from jax.experimental.pallas import tpu as pltpu
from jax.sharding import PartitionSpec as P

RMAX = 32
MESH = pl.DeviceIdType.MESH
AHEAD = 2
VMEM_LIMIT = 52 * 1024 * 1024


def tables(samples, bins):
    turns = (np.arange(bins)[:, None] + 1) * np.arange(samples)[None, :] % samples
    angles = turns.astype(np.float32) * np.float32(2.0 * math.pi / samples)
    return np.stack([np.cos(angles), -np.sin(angles)], axis=1).astype(np.float32)


def round_up(value, unit):
    return -(-value // unit) * unit


def row_messages(n_rows):
    known, messages = [0], []
    for bit in reversed(range(n_rows.bit_length() - 1)):
        messages += [(1 << bit, off) for off in known]
        known += [off ^ (1 << bit) for off in known]
    return messages


def spectra_kernel(nf, n_rows, chunks, x_ref, w_in, t_ref, w_ref, xbuf, sv, spec, land,
                   in_sem, w_sem, s1_send, s1_recv, h_send, h_recv):
    z, r = lax.axis_index("freq"), lax.axis_index("rows")
    width, members = xbuf.shape[1], xbuf.shape[2]
    samples = xbuf.shape[3]
    lanes = w_ref.shape[1]
    sources = width * chunks
    messages = row_messages(n_rows)
    pair = 2 * members

    w_load = pltpu.make_async_copy(w_in, w_ref, w_sem)
    w_load.start()
    loads = []
    for c in range(chunks):
        load = pltpu.make_async_copy(x_ref.at[pl.ds(c * width, width)], xbuf.at[c], in_sem.at[c])
        loads.append(load)
    ahead = min(AHEAD, chunks)
    for c in range(ahead):
        loads[c].start()

    barrier = pltpu.get_barrier_semaphore()
    bits = [1 << b for b in range(n_rows.bit_length() - 1)]
    for d in range(1, nf):
        pl.semaphore_signal(barrier, inc=1, device_id={"freq": lax.rem(z + d, nf)}, device_id_type=MESH)
    for bit in bits:
        flip = r + bit - 2 * bit * lax.rem(r // bit, 2)
        pl.semaphore_signal(barrier, inc=1, device_id={"rows": flip}, device_id_type=MESH)
    pl.semaphore_wait(barrier, nf - 1 + len(bits))

    def flipped(index, mask):
        for bit in bits:
            if mask & bit:
                index = index + bit - 2 * bit * lax.rem(index // bit, 2)
        return index

    def band_copy(c, d):
        to = lax.rem(z + d, nf)
        return pltpu.make_async_remote_copy(
            src_ref=spec.at[c, to], dst_ref=land.at[c, r, z],
            send_sem=s1_send.at[c, d], recv_sem=s1_recv.at[c, d],
            device_id={"freq": to}, device_id_type=MESH)

    def row_copy(c, m, d):
        bit, off = messages[m]
        block = land.at[c, flipped(r, off), lax.rem(z - d + nf, nf)]
        return pltpu.make_async_remote_copy(
            src_ref=block, dst_ref=block,
            send_sem=h_send.at[c, m, d], recv_sem=h_recv.at[c, m, d],
            device_id={"rows": flipped(r, bit)}, device_id_type=MESH)

    first_hop = [m for m, (bit, off) in enumerate(messages) if off == 0]

    def compute(c):
        piece = 128
        lane_v = lax.rem(lax.broadcasted_iota(jnp.int32, (piece, 128), 1), members)
        for s0 in range(0, width, piece):
            block = xbuf[c, s0:s0 + piece].reshape(piece * members, samples)
            found = jnp.dot(block, w_ref[...], preferred_element_type=jnp.float32)
            for tile in range(lanes // 128):
                sv[tile] = found[:, tile * 128:(tile + 1) * 128]
                picked = sv[tile, pl.ds(0, piece, stride=members), :]
                for v in range(1, members):
                    picked = jnp.where(lane_v == v, sv[tile, pl.ds(v, piece, stride=members), :], picked)
                turned = picked.T
                per_tile = 128 // pair
                for f in range(tile * per_tile, min(nf, (tile + 1) * per_tile)):
                    here = (f - tile * per_tile) * pair
                    spec[c, f, :, s0:s0 + piece] = turned[here:here + pair]
        land[c, r, z] = spec[c, z]
        for d in range(1, nf):
            band_copy(c, d).start()
        for m in first_hop:
            row_copy(c, m, 0).start()

    def turn(c):
        for zz in range(nf):
            parts = [land[c, rr, zz] for rr in range(n_rows)]
            again = []
            for part in parts:
                again += [-part[members:], part[:members]]
            full = jnp.concatenate(parts + again, axis=0)
            t_ref[zz * sources + c * width:zz * sources + (c + 1) * width, :] = full.T

    depth = len(bits)
    order = list(reversed(bits))
    forward = [[m for m, (bit, off) in enumerate(messages) if off and (off & -off) == order[k]] for k in range(depth)]

    def stage(k, c):
        if k == 0:
            for d in range(1, nf):
                band_copy(c, d).wait_recv()
                for m in first_hop:
                    row_copy(c, m, d).start()
            return
        for d in range(nf):
            for m, (bit, off) in enumerate(messages):
                if bit == order[k - 1]:
                    row_copy(c, m, d).wait_recv()
            for m in forward[k - 1]:
                row_copy(c, m, d).start()

    w_load.wait()
    for step in range(chunks + depth + 3):
        if step < chunks:
            loads[step].wait()
            compute(step)
            if step + ahead < chunks:
                loads[step + ahead].start()
        for k in range(depth + 1):
            c = step - 2 - (k + 1 if k else 0)
            if 0 <= c < chunks:
                stage(k, c)
                if k == depth:
                    turn(c)
    for c in range(chunks):
        for d in range(nf):
            if d:
                band_copy(c, d).wait_send()
            for m in range(len(messages)):
                row_copy(c, m, d).wait_send()


def project_kernel(t_ref, smap, ranks, right, o_ref, cols, rbuf, proj, r_sem):
    slab = cols.shape[0]
    tile_rows, blocks = ranks.shape[1], ranks.shape[2]
    capacity, tile = right.shape[3], right.shape[4]
    loads_r = [[pltpu.make_async_copy(right.at[c, 0, i], rbuf.at[c, i, pl.ds(0, capacity)], r_sem.at[c, i])
                for i in range(tile_rows)] for c in range(2)]
    for i in range(tile_rows):
        for c in range(2):
            loads_r[c][i].start()
    proj[...] = jnp.zeros_like(proj)

    @pl.loop(0, slab // 32)
    def _(g):
        for u in range(32):
            q = g * 32 + u
            cols[pl.ds(q, 1), :] = t_ref[pl.ds(smap[q], 1), :]

    for i in range(tile_rows):
        for c in range(2):
            loads_r[c][i].wait()
    lane = lax.broadcasted_iota(jnp.int32, (tile_rows * RMAX, 128), 1)
    sign = jnp.where(lane < 64, -1.0, 1.0)
    starts = [jnp.int32(0)] * tile_rows
    for j in range(blocks):
        col = cols[j * tile:(j + 1) * tile, :].astype(jnp.bfloat16)
        at = [pl.multiple_of(s, 8) for s in starts]
        both = [jnp.concatenate([rbuf[c, i, pl.ds(at[i], RMAX), :] for i in range(tile_rows)], axis=0)
                .astype(jnp.bfloat16) for c in range(2)]
        first = jnp.dot(both[0], col, preferred_element_type=jnp.float32)
        second = jnp.dot(both[1], col, preferred_element_type=jnp.float32)
        total = first + sign * pltpu.roll(second, 64, 1)
        for i in range(tile_rows):
            proj[i, pl.ds(at[i], RMAX), :] = total[i * RMAX:(i + 1) * RMAX]
            starts[i] = starts[i] + ranks[0, i, j]
    for i in range(tile_rows):
        proj[i, pl.ds(pl.multiple_of(starts[i], 8), RMAX), :] = jnp.zeros((RMAX, 128), jnp.float32)
    for i in range(tile_rows):
        o_ref[i] = proj[i, :capacity, :]


def image_kernel(nf, p_ref, rmap, left, o_ref, lbuf, img, even, odd, out, l_sem, own_sem, send_sem, recv_sem):
    z = lax.axis_index("freq")
    tile_rows, tile = lbuf.shape[1], lbuf.shape[2]
    receivers = img.shape[0]
    pairs = out.shape[1]
    loads_l = [[pltpu.make_async_copy(left.at[c, 0, i], lbuf.at[c, i], l_sem.at[c, i])
                for i in range(tile_rows)] for c in range(2)]
    for i in range(tile_rows):
        for c in range(2):
            loads_l[c][i].start()
    barrier = pltpu.get_barrier_semaphore()
    for d in range(1, nf):
        pl.semaphore_signal(barrier, inc=1, device_id={"freq": lax.rem(z + d, nf)}, device_id_type=MESH)
    for i in range(tile_rows):
        p = p_ref[i]
        high = p.astype(jnp.bfloat16)
        low = (p - high.astype(jnp.float32)).astype(jnp.bfloat16)
        wide = jnp.concatenate([high, low], axis=1)
        sums = []
        for c in range(2):
            loads_l[c][i].wait()
            prod = jnp.dot(lbuf[c, i].astype(jnp.bfloat16), wide, preferred_element_type=jnp.float32)
            sums.append(prod[:, :128] + prod[:, 128:])
        img[i * tile:(i + 1) * tile, :] = sums[0] + pltpu.roll(sums[1], 64, 1)
    pl.semaphore_wait(barrier, nf - 1)

    copies = []
    lane2 = lax.broadcasted_iota(jnp.int32, (pairs, 128), 1)
    for d in list(range(1, nf)) + [0]:
        to = lax.rem(z + d, nf)
        first = to * 2 * pairs

        @pl.loop(0, pairs // 8)
        def _(g):
            for u in range(8):
                n = first + g * 16 + 2 * u
                even[d, pl.ds(g * 8 + u, 1), :] = img[pl.ds(lax.rem(rmap[n], receivers), 1), :]
                odd[d, pl.ds(g * 8 + u, 1), :] = img[pl.ds(lax.rem(rmap[n + 1], receivers), 1), :]

        out[d] = jnp.where(lane2 < 64, even[d], pltpu.roll(odd[d], 64, 1))
        if d:
            copy = pltpu.make_async_remote_copy(
                src_ref=out.at[d], dst_ref=o_ref.at[z],
                send_sem=send_sem.at[d], recv_sem=recv_sem.at[d],
                device_id={"freq": to}, device_id_type=MESH)
        else:
            copy = pltpu.make_async_copy(out.at[0], o_ref.at[z], own_sem)
        copy.start()
        copies.append(copy)
    for copy in copies:
        copy.wait()


def waves_kernel(nf, members, x_ref, w_ref, o_ref, rows, lhs):
    pairs = x_ref.shape[1]
    wide = w_ref.shape[0]
    groups = members // 8
    lane = lax.broadcasted_iota(jnp.int32, (pairs, 128), 1)
    units = [(part, f) for part in (0, 0, 1) for f in range(nf)]
    pieces = []
    for f in range(nf):
        x = x_ref[f]
        high = x.astype(jnp.bfloat16).astype(jnp.float32)
        pieces.append((high, x - high))
    for parity in range(2):
        for g in range(groups):
            base = 64 * parity + 16 * g
            for tile in range(wide // 128):
                acc = jnp.zeros((pairs, 128), jnp.float32)
                for slot, (part, f) in enumerate(units[tile * 8:tile * 8 + 8]):
                    shift = (16 * slot - base) % 128
                    value = pieces[f][part]
                    if shift:
                        value = pltpu.roll(value, shift, 1)
                    acc = jnp.where(lane // 16 == slot, value, acc)
                rows[parity, g, :, tile * 128:tile * 128 + 128] = acc
    sub = lax.broadcasted_iota(jnp.int32, (8, wide), 0)
    keep = lax.rem(lax.broadcasted_iota(jnp.int32, (8, wide), 1), 8) == sub
    half = pairs * members
    cut = min(256, w_ref.shape[1])
    for first in (0, pairs):
        for n in range(first, first + pairs):
            parts = []
            for g in range(groups):
                row = rows[n % 2, g, pl.ds(n // 2, 1), :]
                parts.append(jnp.where(keep, jnp.broadcast_to(row, (8, wide)), 0.0))
            lhs[n * members:(n + 1) * members, :] = jnp.concatenate(parts, axis=0).astype(jnp.bfloat16)
        block = lhs[first * members:first * members + half, :]
        for t in range(0, w_ref.shape[1], cut):
            out = jnp.dot(block, w_ref[:, t:t + cut], preferred_element_type=jnp.float32)
            o_ref[0, first:first + pairs, :, t:t + cut] = out.astype(jnp.bfloat16).reshape(pairs, members, cut)


def per_device(traces, tile_ranks, source_map, receiver_map, left_factors, right_factors):
    sources, members, samples = traces.shape
    nf, n_rows = lax.axis_size("freq"), lax.axis_size("rows")
    slab = source_map.shape[0]
    receivers = receiver_map.shape[0]
    all_members = members * n_rows
    tile_rows, capacity, tile = right_factors.shape[2:]
    chunks = max(1, sources // 512)
    width = sources // chunks
    basis = tables(samples, nf)

    forward = (basis / np.float32(math.sqrt(samples))).astype(jnp.bfloat16)
    lanes = round_up(2 * nf * members, 128)
    w = np.zeros((samples, lanes), jnp.bfloat16)
    w[:, :2 * nf * members] = np.repeat(forward.reshape(2 * nf, samples), members, axis=0).T
    n_msg = n_rows - 1
    turned = pl.pallas_call(
        functools.partial(spectra_kernel, nf, n_rows, chunks),
        out_shape=jax.ShapeDtypeStruct((slab, 128), jnp.float32),
        in_specs=[pl.BlockSpec(memory_space=pl.ANY)] * 2,
        out_specs=pl.BlockSpec(memory_space=pltpu.VMEM),
        scratch_shapes=[
            pltpu.VMEM((samples, lanes), jnp.bfloat16),
            pltpu.VMEM((chunks, width, members, samples), jnp.bfloat16),
            pltpu.VMEM((lanes // 128, 128 * members, 128), jnp.float32),
            pltpu.VMEM((chunks, nf, 2 * members, width), jnp.float32),
            pltpu.VMEM((chunks, n_rows, nf, 2 * members, width), jnp.float32),
            pltpu.SemaphoreType.DMA((chunks,)),
            pltpu.SemaphoreType.DMA(()),
            pltpu.SemaphoreType.DMA((chunks, nf)),
            pltpu.SemaphoreType.DMA((chunks, nf)),
            pltpu.SemaphoreType.DMA((chunks, n_msg, nf)),
            pltpu.SemaphoreType.DMA((chunks, n_msg, nf)),
        ],
        compiler_params=pltpu.CompilerParams(
            collective_id=0, has_side_effects=True, vmem_limit_bytes=VMEM_LIMIT),
        name="spectra",
    )(traces, jnp.asarray(w))

    per = receivers // nf
    projected = pl.pallas_call(
        project_kernel,
        out_shape=jax.ShapeDtypeStruct((tile_rows, capacity, 128), jnp.float32),
        in_specs=[
            pl.BlockSpec(memory_space=pltpu.VMEM),
            pl.BlockSpec(memory_space=pltpu.SMEM),
            pl.BlockSpec(memory_space=pltpu.SMEM),
            pl.BlockSpec(memory_space=pl.ANY),
        ],
        out_specs=pl.BlockSpec(memory_space=pltpu.VMEM),
        scratch_shapes=[
            pltpu.VMEM((slab, 128), jnp.float32),
            pltpu.VMEM((2, tile_rows, capacity + RMAX, tile), jnp.float32),
            pltpu.VMEM((tile_rows, capacity + RMAX, 128), jnp.float32),
            pltpu.SemaphoreType.DMA((2, tile_rows)),
        ],
        compiler_params=pltpu.CompilerParams(vmem_limit_bytes=VMEM_LIMIT),
        name="project",
    )(turned, source_map, tile_ranks, right_factors)

    pairs = per // 2
    returned = pl.pallas_call(
        functools.partial(image_kernel, nf),
        out_shape=jax.ShapeDtypeStruct((nf, pairs, 128), jnp.float32),
        in_specs=[
            pl.BlockSpec(memory_space=pltpu.VMEM),
            pl.BlockSpec(memory_space=pltpu.SMEM),
            pl.BlockSpec(memory_space=pl.ANY),
        ],
        out_specs=pl.BlockSpec(memory_space=pl.ANY),
        scratch_shapes=[
            pltpu.VMEM((2, tile_rows, tile, capacity), jnp.float32),
            pltpu.VMEM((receivers, 128), jnp.float32),
            pltpu.VMEM((nf, pairs, 128), jnp.float32),
            pltpu.VMEM((nf, pairs, 128), jnp.float32),
            pltpu.VMEM((nf, pairs, 128), jnp.float32),
            pltpu.SemaphoreType.DMA((2, tile_rows)),
            pltpu.SemaphoreType.DMA(()),
            pltpu.SemaphoreType.DMA((nf,)),
            pltpu.SemaphoreType.DMA((nf,)),
        ],
        compiler_params=pltpu.CompilerParams(
            collective_id=1, has_side_effects=True, vmem_limit_bytes=VMEM_LIMIT),
        name="image",
    )(projected, receiver_map, left_factors)

    inverse = (basis / np.float32(math.sqrt(nf))).astype(np.float32)
    high = inverse.astype(jnp.bfloat16)
    low = (inverse - high.astype(np.float32)).astype(jnp.bfloat16)
    wide = round_up(3 * nf * 16, 128)
    wb = np.zeros((wide, samples), jnp.bfloat16)
    for part, table in enumerate((high, low, high)):
        wb[part * nf * 16:(part + 1) * nf * 16] = np.repeat(table.reshape(2 * nf, samples), 8, axis=0)
    nb = min(64, per)
    return pl.pallas_call(
        functools.partial(waves_kernel, nf, all_members),
        grid=(per // nb,),
        out_shape=jax.ShapeDtypeStruct((1, per, all_members, samples), jnp.bfloat16),
        in_specs=[
            pl.BlockSpec((nf, nb // 2, 128), lambda i: (0, i, 0)),
            pl.BlockSpec((wide, samples), lambda i: (0, 0)),
        ],
        out_specs=pl.BlockSpec((1, nb, all_members, samples), lambda i: (0, i, 0, 0)),
        scratch_shapes=[
            pltpu.VMEM((2, all_members // 8, nb // 2, wide), jnp.float32),
            pltpu.VMEM((nb * all_members, wide), jnp.bfloat16),
        ],
        compiler_params=pltpu.CompilerParams(vmem_limit_bytes=VMEM_LIMIT),
        name="waves",
    )(returned, jnp.asarray(wb))


def solution(mesh):
    return jax.shard_map(
        per_device,
        mesh=mesh,
        in_specs=(
            P(("groups", "freq"), "rows", None),
            P(("groups", "freq"), "rows", None),
            P("groups"),
            P(("groups", "rows")),
            P(None, ("groups", "freq"), "rows", None, None),
            P(None, ("groups", "freq"), "rows", None, None),
        ),
        out_specs=P(("groups", "rows"), "freq", None, None),
        check_vma=False,
    )
```
